256 devices in a mesh: occ: 2 (over z_hi), vir: 32 (over z_lo, x, core), pair: 4 (over y).
Axes of the slice: x: 4, y: 4, z: 8 (z_hi: 2, z_lo: 4; z = z_hi * 4 + z_lo), core: 2. Of those that a mesh axis runs over, the one named last changes fastest.
Arguments:
- amplitudes: bfloat16 [2, 1280, 128, 1280], P(None, 'pair', 'vir', 'occ'), may hold values from -6 to 6
- integrals: bfloat16 [128, 1280, 2, 1280], P('vir', 'occ', None, 'pair'), may hold values from -0.01953125 to 0.01953125
- screen: int32 [2, 20, 128, 20], P(None, 'pair', 'vir', 'occ'), may hold values 0 or 1
- occ_energy: float32 [2], replicated, may hold values from -2 to -0.5
- vir_energy: float32 [1280], replicated, may hold values from 0.5 to 3
- owner: int32 [4], replicated, may hold values from 0 to 3, as said below
Outputs:
- residual: float32 [4, 1280, 1280], P('pair', ('occ', 'vir'))
The draws below stay inside these ranges and needn't reach their ends.
Inputs may be any that keep to these rules, and one draw needn't show every extreme that they name: owner names every ordered pair i * 2 + j once; for i != j the slot of (j, i) is that of (i, j) plus 4 // 2, counted modulo 4.
All inputs are finite; a program needn't handle non-finite values. No bound on the sum of `screen` on one device may be relied on, other than what follows from the above.
Results may differ from the reference program's by a relative error of at most 0.0003.
Values may be sent and summed in bfloat16 or wider, within the bound.
No kernel may reach another device: no remote copies, remote signals or barrier semaphores. Data moves between devices by JAX's collectives and lax.ppermute only.
A program may use at most 128 MiB of HBM per device.

```python
import jax
import jax.numpy as jnp

BATCH_OCC = 2
OCC = 128
VIR = 1280
TILE = 64
VTILES = 20
PAIRS = 4


def draw_owner(key, part):
    key = jax.random.fold_in(key, 7)
    start_key, order_key, diag_key = jax.random.split(key, 3)
    start = jax.random.randint(start_key, (), 0, 4).astype(jnp.int32)
    order = jax.random.randint(order_key, (), 0, 2).astype(jnp.int32)
    diag_order = jax.random.randint(diag_key, (), 0, 2).astype(jnp.int32)
    slots = jnp.arange(PAIRS, dtype=jnp.int32)
    place = (slots - start + PAIRS) % PAIRS
    values = jnp.where(place == 0, 1 + order, jnp.where(place == 2, 2 - order, jnp.where(place == 1, 3 * diag_order, 3 - 3 * diag_order)))
    return values.astype(jnp.int32)


def place_ends(drawn, key, low, largest):
    spot = [jax.random.randint(jax.random.fold_in(key, axis), (), 0, length) for axis, length in enumerate(drawn.shape)]
    main_axis = drawn.shape.index(max(drawn.shape))
    next_to = spot[:main_axis] + [(spot[main_axis] + 1) % drawn.shape[main_axis]] + spot[main_axis + 1:]
    return drawn.at[tuple(spot)].set(low).at[tuple(next_to)].set(largest)


def strengthened(array, key, source, target, blocks, factor):
    owner, partner = [(jnp.arange(array.shape[dim]) // (array.shape[dim] // blocks)).reshape([-1 if axis == dim else 1 for axis in range(array.ndim)]) for dim in (source, target)]
    chosen = jax.random.permutation(key, blocks)[partner]
    strong = (owner == chosen) | (owner == (partner + blocks // 2) % blocks)
    return jnp.where(strong, factor * array, array)


def levels(own_key, extent, cuts, smallest, high):
    loudness, own = 1.0, jax.random.fold_in(own_key, 6)
    for axis_at, parts in cuts:
        heights = jnp.exp(jax.random.uniform(jax.random.fold_in(own, axis_at), (parts,), jnp.float32, smallest / len(cuts), high / len(cuts)))
        loudness = loudness * jnp.repeat(heights, extent[axis_at] // parts).reshape([-1 if axis == axis_at else 1 for axis in range(len(extent))])
    return loudness


def noise(stream_key, extent, width, reach, shards=(), held_as=jnp.bfloat16):
    result = width * jax.random.normal(stream_key, extent, jnp.float32)
    if shards:
        result = result * levels(stream_key, extent, shards, -0.22, 0.18)
    return jnp.clip(result, -reach, reach).astype(held_as)


def heavy_noise(own_key, shape, deviation, bound, cuts, heavy, kind=jnp.bfloat16):
    entries = deviation * jax.random.normal(own_key, shape, jnp.float32)
    if cuts:
        entries = entries * levels(own_key, shape, cuts, -0.22, 0.18)
    return jnp.clip(strengthened(entries, jax.random.fold_in(own_key, 3), *heavy), -bound, bound).astype(kind)


def setup_inputs(seed: int = 0) -> dict:
    key_list = jax.random.split(jax.random.key(seed), 7)
    amplitudes = heavy_noise(key_list[0], (BATCH_OCC, VIR, OCC, VIR), 1.0, 6.0, ((1, 4), (2, 32), (3, 2)), (2, 1, 32, 2.75))
    integrals = noise(key_list[1], (OCC, VIR, BATCH_OCC, VIR), (OCC * VIR // 2) ** -0.5, 0.01953125, ((0, 32), (1, 2), (3, 4)))
    screen = place_ends((jax.random.randint(key_list[2], (BATCH_OCC, VTILES, OCC, VTILES), 0, 2) < 1).astype(jnp.int32), jax.random.fold_in(key_list[2], 1), 0, 1)
    occ_energy = jnp.clip(jax.random.uniform(key_list[3], (BATCH_OCC,), jnp.float32, -2.0, -0.5), -2.0, -0.5)
    vir_energy = jnp.clip(jax.random.uniform(key_list[4], (VIR,), jnp.float32, 0.5, 3.0), 0.5, 3.0)
    owner = draw_owner(jax.random.fold_in(key_list[6], 71), 0)
    return dict(amplitudes=amplitudes, integrals=integrals, screen=screen, occ_energy=occ_energy, vir_energy=vir_energy, owner=owner)


def reference(amplitudes, integrals, screen, occ_energy, vir_energy, owner):
    right_side = integrals.reshape(OCC * VIR, BATCH_OCC * VIR)
    blocks_all = []
    for occ_index in range(BATCH_OCC):
        tile_mask = jnp.repeat(jnp.repeat(screen[occ_index], TILE, axis=0), TILE, axis=2)
        screened = amplitudes[occ_index] * tile_mask.astype(jnp.bfloat16)
        product = jnp.dot(screened.reshape(VIR, OCC * VIR), right_side, preferred_element_type=jnp.float32)
        blocks_all.append(product.reshape(VIR, BATCH_OCC, VIR))
    cycle = jnp.stack(blocks_all)
    first_occ = owner // BATCH_OCC
    second_occ = owner % BATCH_OCC
    direct = cycle[first_occ, :, second_occ, :]
    mirrored = jnp.swapaxes(cycle[second_occ, :, first_occ, :], 1, 2)
    energy_gap = (occ_energy[first_occ][:, None, None] + occ_energy[second_occ][:, None, None]
                  - vir_energy[None, :, None] - vir_energy[None, None, :])
    return (direct + mirrored) / energy_gap
```

```python
import functools

import jax
import jax.numpy as jnp
from jax import lax
from jax.experimental import pallas as pl
from jax.experimental.pallas import tpu as pltpu
from jax.sharding import Mesh, PartitionSpec as P

AXES = ("zh", "zm", "zp", "x", "core", "y")
Z = ("zh", "zm", "zp")
ALL = ("zh", "zm", "zp", "x", "core")
GROUPS = ((0, 2), (2, 4), (4, 5))
F32 = jnp.float32


def permute(value, axis, target):
    return lax.ppermute(value, axis, [(s, target(s)) for s in range(lax.axis_size(axis))])


def product_kernel(jobs, n_left, n_right, core_ref, *refs):
    left = refs[:n_left]
    right = refs[n_left : n_left + n_right]
    keep_ref, send_ref = refs[n_left + n_right :]
    me = core_ref[0]
    for li, ri, base in jobs:
        a_ref, b_ref = left[li], right[ri]
        chunks, depth = a_ref.shape[0], a_ref.shape[1]
        tiles = b_ref.shape[1] // 128

        def step(n, carry, a_ref=a_ref, b_ref=b_ref, depth=depth, tiles=tiles, base=base):
            acc = None
            for k in range(depth):
                part = lax.dot_general(
                    a_ref[n, k], b_ref[k], (((1,), (1,)), ((), ())), preferred_element_type=F32
                )
                acc = part if acc is None else acc + part
            low, high = acc[:64], acc[64:]
            keep = jnp.where(me == 0, low, high)
            send = jnp.where(me == 0, high, low)
            for c in range(tiles):
                at = base + n * tiles + c
                span = slice(c * 128, (c + 1) * 128)
                keep_ref[:, at] = keep[:, span].reshape(4, 16, 128)
                send_ref[:, at] = send[:, span].reshape(4, 16, 128)
            return carry

        lax.fori_loop(0, chunks, step, 0)


def product(core, left, right, pairs):
    jobs, base, flops = [], 0, 0
    for li, ri in pairs:
        jobs.append((li, ri, base))
        count = left[li].shape[0] * (right[ri].shape[1] // 128)
        base += count
        flops += count * 2 * 128 * 128 * 2560
    size = sum(v.size * 2 for v in left + right) + base * 65536
    half = jax.ShapeDtypeStruct((4, base, 16, 128), F32)
    vmem = pl.BlockSpec(memory_space=pltpu.VMEM)
    return pl.pallas_call(
        functools.partial(product_kernel, jobs, len(left), len(right)),
        out_shape=(half, half),
        in_specs=[pl.BlockSpec(memory_space=pltpu.SMEM)] + [vmem] * (len(left) + len(right)),
        out_specs=(vmem, vmem),
        compiler_params=pltpu.CompilerParams(vmem_limit_bytes=40 * 2**20),
        cost_estimate=pl.CostEstimate(flops=flops, bytes_accessed=size, transcendentals=0),
    )(core, *left, *right)


def reduce_chip_x(keep, send):
    got = permute(send, "core", lambda s: 1 - s)
    mine = lax.axis_index("x")
    parts = []
    for r in range(4):
        at = (mine + r) % 4
        parts.append(
            lax.dynamic_index_in_dim(keep, at, 0, keepdims=False)
            + lax.dynamic_index_in_dim(got, at, 0, keepdims=False)
        )
    total = parts[0]
    for r in (1, 2, 3):
        total = total + permute(parts[r], "x", lambda s, r=r: (s + r) % 4)
    return total


def reduce_z(pieces):
    value = jnp.concatenate(pieces, axis=0)
    tiles = value.shape[0]
    value = value.reshape(tiles, 2, 2, 4, 128).transpose(3, 2, 0, 1, 4).reshape(8, tiles * 2, 128)
    value = lax.all_to_all(value, Z, split_axis=0, concat_axis=0, tiled=True)
    return jnp.sum(value, axis=0).reshape(tiles, 2, 128)


def body(amplitudes, integrals, screen, occ_energy, vir_energy, owner):
    k_local = amplitudes.shape[2]
    p = lax.axis_index("y")
    core = lax.axis_index("core").astype(jnp.int32).reshape(1)
    mask = jnp.repeat(screen, 64, axis=3).astype(jnp.bfloat16)
    masked = amplitudes.reshape(2, 5, 64, 4, 640) * mask[:, :, None]
    masked = masked.reshape(2, 2, 4, 2, 5, 4, 4, 640).transpose(4, 6, 3, 2, 0, 1, 5, 7)
    own_left = masked.reshape(5, k_local, 128, 640)
    own_right = integrals.transpose(0, 2, 3, 1).reshape(k_local, 640, 640)

    far_left, far_right = [], []
    for lo, hi in GROUPS:
        far_right.append(permute(own_right[:, lo * 128 : hi * 128], "y", lambda s: 3 - s))
        far_left.append(permute(own_left[lo:hi], "y", lambda s: s ^ 1))

    reduced, where = [], []

    def record(rows, cols):
        for rs, rt in rows:
            for cs, ct in cols:
                where.append((rs, rt, cs, ct))

    own = [(0, t) for t in range(5)]
    far = [[(1, t) for t in range(lo, hi)] for lo, hi in GROUPS]
    record(own, own)
    reduced.append(reduce_chip_x(*product(core, [own_left], [own_right], [(0, 0)])))
    for g in range(len(GROUPS)):
        left = [own_left] + far_left[: g + 1]
        right = [own_right] + far_right[: g + 1]
        names_l = [own] + far[: g + 1]
        names_r = [own] + far[: g + 1]
        pairs = [(g + 1, r) for r in range(g + 2)] + [(l, g + 1) for l in range(g + 1)]
        for l, r in pairs:
            record(names_l[l], names_r[r])
        reduced.append(reduce_chip_x(*product(core, left, right, pairs)))

    done = [reduce_z(reduced[:2]), reduce_z(reduced[2:])]
    tiles = jnp.concatenate(done, axis=0)
    place = {w: n for n, w in enumerate(where)}
    blocks = []
    for rs in range(2):
        for rt in range(5):
            row = [tiles[place[(rs, rt, cs, ct)]] for cs in range(2) for ct in range(5)]
            blocks.append(jnp.concatenate(row, axis=1))
    full = jnp.stack(blocks).reshape(2, 5, 2, 2, 2, 320)

    chunks = []
    for q in range(4):
        rows = jnp.where(p == q, full[0], full[1])
        for s in range(4):
            i, j = owner[s] // 2, owner[s] % 2
            pair = []
            for u, v in ((i, j), (j, i)):
                picked = lax.dynamic_index_in_dim(rows, u, 1, keepdims=False)
                picked = lax.dynamic_index_in_dim(picked, v, 2, keepdims=False)
                pair.append(picked.reshape(5, 640))
            chunks.append(jnp.stack(pair))
    sent = jnp.stack(chunks).reshape(16, 10, 640)
    got = lax.all_to_all(sent, ("zh", "zm", "y"), split_axis=0, concat_axis=0, tiled=True)
    got = got.reshape(4, 4, 2, 5, 2, 320)
    lower = [(0, 0), (1, 0), (1, 1), (0, 1)]
    upper = [(3, 1), (2, 1), (2, 0), (3, 0)]
    is_low = lax.axis_index("zh") == 0
    quarters = [
        jnp.where(is_low, got[:, a[0], :, :, a[1]], got[:, b[0], :, :, b[1]])
        for a, b in zip(lower, upper)
    ]
    rows = jnp.stack(quarters, axis=3)
    rows = rows.transpose(1, 2, 0, 3, 4).reshape(2, 20, 1280)
    direct, swapped = rows[0], rows[1]
    mirrored = lax.all_to_all(swapped, ALL, split_axis=1, concat_axis=0, tiled=True).T

    combo = owner[p]
    first, second = combo // 2, combo % 2
    row_energy = lax.dynamic_slice_in_dim(vir_energy, lax.axis_index(ALL) * 20, 20)
    gap = occ_energy[first] + occ_energy[second] - row_energy[:, None] - vir_energy[None, :]
    return ((direct + mirrored) / gap)[None]


def solution(mesh):
    fine = Mesh(mesh.devices.reshape(2, 2, 2, 4, 2, 4), AXES)
    vir = ("zm", "zp", "x", "core")
    return jax.shard_map(
        body,
        mesh=fine,
        in_specs=(
            P(None, "y", vir, "zh"),
            P(vir, "zh", None, "y"),
            P(None, "y", vir, "zh"),
            P(),
            P(),
            P(),
        ),
        out_specs=P("y", ALL, None),
        check_vma=False,
    )
```

```python
import functools

import jax
import jax.numpy as jnp
from jax import lax
from jax.experimental import pallas as pl
from jax.experimental.pallas import tpu as pltpu
from jax.sharding import Mesh, PartitionSpec as P

AXES = ("zh", "zm", "zp", "x", "core", "y")
Z = ("zh", "zm", "zp")
ALL = ("zh", "zm", "zp", "x", "core")
F32 = jnp.float32


def permute(value, axis, target):
    return lax.ppermute(value, axis, [(s, target(s)) for s in range(lax.axis_size(axis))])


def prepare_kernel(chunks, mask_ref, rows_ref, out_ref):
    for n, t in enumerate(chunks):

        @pl.when(pl.program_id(0) == n)
        def _(t=t):
            for x in range(4):
                for core in range(2):
                    group = []
                    for i in range(2):
                        for zp in range(2):
                            tile = (zp * 160 + (x * 2 + core) * 20 + 4 * t) // 64
                            value = rows_ref[i, zp, x * 2 + core, 0] * mask_ref[i, tile][None]
                            group.append(value.astype(F32))
                    value = jnp.transpose(jnp.concatenate(group, 0), (1, 0, 2))
                    value = value.astype(jnp.bfloat16)
                    at = core * 64 + x * 16
                    for k in range(value.shape[0]):
                        out_ref[0, k, at : at + 16, :] = value[k]


def prepare(amplitudes, mask, lo, hi):
    return pl.pallas_call(
        functools.partial(prepare_kernel, tuple(range(lo, hi))),
        grid=(hi - lo,),
        out_shape=jax.ShapeDtypeStruct((hi - lo, 4, 128, 640), jnp.bfloat16),
        in_specs=[
            pl.BlockSpec((2, 5, 4, 640), lambda t: (0, 0, 0, 0)),
            pl.BlockSpec((2, 2, 8, 1, 4, 4, 640), lambda t: (0, 0, 0, t + lo, 0, 0, 0)),
        ],
        out_specs=pl.BlockSpec((1, 4, 128, 640), lambda t: (t, 0, 0, 0)),
        compiler_params=pltpu.CompilerParams(vmem_limit_bytes=40 * 2**20),
        cost_estimate=pl.CostEstimate(flops=1, bytes_accessed=1, transcendentals=0),
    )(mask, amplitudes.reshape(2, 2, 8, 5, 4, 4, 640))


def product_kernel(jobs, n_left, n_right, core_ref, *refs):
    left = refs[:n_left]
    right = refs[n_left : n_left + n_right]
    keep_ref, send_ref = refs[n_left + n_right :]
    me = core_ref[0]
    for li, ri, base in jobs:
        a_ref, b_ref = left[li], right[ri]
        chunks, depth = a_ref.shape[0], a_ref.shape[1]
        columns = b_ref.shape[1]
        for start in range(0, columns, 256):
            width = min(256, columns - start)
            acc = None
            for k in range(depth):
                part = lax.dot_general(
                    a_ref[:, k].reshape(chunks * 128, a_ref.shape[3]),
                    b_ref[k, start : start + width],
                    (((1,), (1,)), ((), ())),
                    preferred_element_type=F32,
                )
                acc = part if acc is None else acc + part
            acc = acc.reshape(chunks, 2, 4, 16, width)
            low, high = acc[:, 0], acc[:, 1]
            keep = jnp.where(me == 0, low, high)
            send = jnp.where(me == 0, high, low)
            for n in range(chunks):
                for c in range(width // 128):
                    at = base + n * (columns // 128) + start // 128 + c
                    span = slice(c * 128, (c + 1) * 128)
                    keep_ref[:, at] = keep[n, :, :, span]
                    send_ref[:, at] = send[n, :, :, span]


def product(core, left, right, pairs):
    jobs, base = [], 0
    for li, ri in pairs:
        jobs.append((li, ri, base))
        count = left[li].shape[0] * (right[ri].shape[1] // 128)
        base += count
    half = jax.ShapeDtypeStruct((4, base, 16, 128), F32)
    vmem = pl.BlockSpec(memory_space=pltpu.VMEM)
    return pl.pallas_call(
        functools.partial(product_kernel, jobs, len(left), len(right)),
        out_shape=(half, half),
        in_specs=[pl.BlockSpec(memory_space=pltpu.SMEM)] + [vmem] * (len(left) + len(right)),
        out_specs=(vmem, vmem),
        compiler_params=pltpu.CompilerParams(vmem_limit_bytes=40 * 2**20),
        cost_estimate=pl.CostEstimate(flops=1, bytes_accessed=1, transcendentals=0),
    )(core, *left, *right)


def reduce_chip(keep, send):
    got = permute(send, "core", lambda s: 1 - s)
    mine = place_on("x")
    spots = [mine, (mine + 1) & 3, (mine + 2) & 3, (mine + 3) & 3]
    return [take(keep, at) + take(got, at) for at in spots]


def reduce_x(parts):
    moved = [permute(parts[r], "x", lambda s, r=r: (s + r) % 4) for r in (1, 2, 3)]
    return parts[0] + moved[0] + moved[1] + moved[2]


def exchange_ring(parts, axis):
    moved = [parts[0]] + [permute(parts[r], axis, lambda s, r=r: (s + r) % 4) for r in (1, 2, 3)]
    ring = jnp.stack(moved[::-1] + moved[::-1])
    return lax.dynamic_slice_in_dim(ring, 3 - place_on(axis), 4)


def place_on(axis):
    return lax.axis_index(axis).astype(jnp.uint32)


def take(value, at):
    return lax.dynamic_index_in_dim(value, at, 0, keepdims=False)


def tie(first, second):
    return lax.optimization_barrier((first, second))[0]


def reduce_z(total):
    tiles = total.shape[0]
    value = total.reshape(tiles, 2, 2, 2, 2, 128)
    value = value.transpose(2, 4, 3, 0, 1, 5).reshape(2, 2, 2, tiles * 2, 128)
    for axis in Z[::-1]:
        mine = place_on(axis)
        keep, send = take(value, mine), take(value, 1 - mine)
        got = permute(send, axis, lambda s: 1 - s)
        value = keep + got if axis != Z[0] else None
    return keep, got


def assemble_kernel(places, *refs):
    out_ref = refs[-1]
    for n, place in enumerate(places):
        keep_ref, got_ref = refs[2 * n : 2 * n + 2]
        for m, (rs, rt, cs, ct) in enumerate(place):
            at = (cs * 5 + ct) * 128
            for i in range(2):
                row = slice(2 * m + i, 2 * m + i + 1)
                value = keep_ref[row, :] + got_ref[row, :]
                out_ref[i, rs * 5 + rt : rs * 5 + rt + 1, at : at + 128] = value


def assemble(places, pieces):
    flat = [v for pair in pieces for v in pair]
    vmem = pl.BlockSpec(memory_space=pltpu.VMEM)
    return pl.pallas_call(
        functools.partial(assemble_kernel, places),
        out_shape=jax.ShapeDtypeStruct((2, 10, 1280), F32),
        in_specs=[vmem] * len(flat),
        out_specs=vmem,
        cost_estimate=pl.CostEstimate(flops=1, bytes_accessed=1, transcendentals=0),
    )(*flat)


def body(amplitudes, integrals, screen, occ_energy, vir_energy, owner):
    core = lax.axis_index("core").astype(jnp.int32).reshape(1)
    mask = jnp.repeat(screen, 64, axis=3).astype(jnp.bfloat16)

    own_right = integrals.transpose(0, 2, 3, 1).reshape(4, 640, 640)
    far_right = permute(own_right, "y", lambda s: 3 - s)
    own_left = prepare(amplitudes, mask, 0, 5)
    far_left = permute(own_left, "y", lambda s: s ^ 1)

    def cells_of(row_source, col_source):
        return [(row_source, r, col_source, c) for r in range(5) for c in range(5)]

    def block(left, right):
        pairs = [(l, r) for l in range(len(left)) for r in range(len(right))]
        keep, send = product(core, left, right, pairs)
        return keep, reduce_chip(keep, send)

    total = reduce_x(block([own_left], [own_right])[1])
    pieces = [reduce_z(total)]
    far_right = tie(far_right, pieces[0][0])
    keep, parts_a = block([own_left], [far_right])
    total_a = reduce_x(parts_a)
    far_left = tie(far_left, keep)
    total_b = reduce_x(block([far_left], [own_right, far_right])[1])
    pieces.append(reduce_z(jnp.concatenate([total_a, total_b])))
    places = [cells_of(0, 0), cells_of(0, 1) + cells_of(1, 0) + cells_of(1, 1)]
    full = assemble(places, pieces)
    full = full.reshape(2, 10, 2, 2, 320)

    turn = (lax.axis_index("y") + jnp.arange(4)) & 3
    combo = jnp.sum(jnp.where(turn[:, None] == jnp.arange(4)[None], owner[None], 0), axis=1)
    wanted = jnp.stack([combo, 2 * (combo & 1) + (combo >> 1)], axis=1)[:, :, None, None]
    by_pair = [full[i, :, :, j].reshape(10, 640) for i in range(2) for j in range(2)]
    got = jnp.where(
        wanted < 2,
        jnp.where(wanted == 0, by_pair[0], by_pair[1]),
        jnp.where(wanted == 2, by_pair[2], by_pair[3]),
    ).reshape(4, 20, 640)
    got = exchange_ring(got, "y").reshape(4, 2, 2, 5, 2, 320)
    cells = (
        ((0, 0), (1, 0), (1, 1), (0, 1)),
        ((3, 1), (2, 1), (2, 0), (3, 0)),
    )
    rows = []
    for q in range(4):
        cols = [
            got[source, :, 0 if source == q else 1, :, side] for source, side in cells[q // 2]
        ]
        rows.append(jnp.concatenate(cols, axis=-1))
    rows = jnp.stack(rows, axis=1)
    swapped = rows[1].reshape(20, 1280)
    swapped = swapped.reshape(20, 64, 20).transpose(1, 0, 2).reshape(64, 400)
    home, swapped = lax.optimization_barrier((rows[0], swapped))
    mirrored = lax.all_to_all(swapped, ALL, split_axis=0, concat_axis=0, tiled=True)
    mirrored = mirrored.reshape(4, 2, 8, 4, 5, 20).transpose(5, 3, 1, 2, 4, 0).reshape(20, 1280)
    me = place_on(("zh", "zm"))
    direct = exchange_ring([take(home, (me + r) & 3) for r in range(4)], ("zh", "zm"))
    direct = direct.transpose(1, 0, 2).reshape(20, 1280)

    mine = combo[:1]
    first = jnp.where(mine < 2, occ_energy[:1], occ_energy[1:])
    second = jnp.where((mine & 1) == 0, occ_energy[:1], occ_energy[1:])
    row_energy = lax.dynamic_slice_in_dim(vir_energy, place_on(ALL) * 20, 20)
    gap = (first + second)[:, None] - row_energy[:, None] - vir_energy[None, :]
    return ((direct + mirrored) / gap)[None]


def solution(mesh):
    fine = Mesh(mesh.devices.reshape(2, 2, 2, 4, 2, 4), AXES)
    vir = ("zm", "zp", "x", "core")
    return jax.shard_map(
        body,
        mesh=fine,
        in_specs=(
            P(None, "y", vir, "zh"),
            P(vir, "zh", None, "y"),
            P(None, "y", vir, "zh"),
            P(),
            P(),
            P(),
        ),
        out_specs=P("y", ALL, None),
        check_vma=False,
    )
```

```python
import functools

import jax
import jax.numpy as jnp
from jax import lax
from jax.experimental import pallas as pl
from jax.experimental.pallas import tpu as pltpu
from jax.sharding import Mesh, PartitionSpec as P

AXES = ("zh", "zm", "zp", "x", "core", "y")
Z = ("zh", "zm", "zp")
ALL = ("zh", "zm", "zp", "x", "core")
F32 = jnp.float32


def permute(value, axis, target):
    return lax.ppermute(value, axis, [(s, target(s)) for s in range(lax.axis_size(axis))])


def prepare_kernel(chunks, mask_ref, rows_ref, out_ref):
    for n, t in enumerate(chunks):

        @pl.when(pl.program_id(0) == n)
        def _(t=t):
            for x in range(4):
                for core in range(2):
                    group = []
                    for i in range(2):
                        for zp in range(2):
                            tile = (zp * 160 + (x * 2 + core) * 20 + 4 * t) // 64
                            value = rows_ref[i, zp, x * 2 + core, 0] * mask_ref[i, tile][None]
                            group.append(value.astype(F32))
                    value = jnp.transpose(jnp.concatenate(group, 0), (1, 0, 2))
                    value = value.astype(jnp.bfloat16)
                    at = core * 64 + x * 16
                    for k in range(value.shape[0]):
                        out_ref[0, k, at : at + 16, :] = value[k]


def prepare(amplitudes, mask, lo, hi):
    return pl.pallas_call(
        functools.partial(prepare_kernel, tuple(range(lo, hi))),
        grid=(hi - lo,),
        out_shape=jax.ShapeDtypeStruct((hi - lo, 4, 128, 640), jnp.bfloat16),
        in_specs=[
            pl.BlockSpec((2, 5, 4, 640), lambda t: (0, 0, 0, 0)),
            pl.BlockSpec((2, 2, 8, 1, 4, 4, 640), lambda t: (0, 0, 0, t + lo, 0, 0, 0)),
        ],
        out_specs=pl.BlockSpec((1, 4, 128, 640), lambda t: (t, 0, 0, 0)),
        compiler_params=pltpu.CompilerParams(vmem_limit_bytes=40 * 2**20),
        cost_estimate=pl.CostEstimate(flops=1, bytes_accessed=1, transcendentals=0),
    )(mask, amplitudes.reshape(2, 2, 8, 5, 4, 4, 640))


def product_kernel(jobs, n_left, n_right, core_ref, *refs):
    left = refs[:n_left]
    right = refs[n_left : n_left + n_right]
    keep_ref, send_ref = refs[n_left + n_right :]
    me = core_ref[0]
    for li, ri, base in jobs:
        a_ref, b_ref = left[li], right[ri]
        chunks, depth = a_ref.shape[0], a_ref.shape[1]
        columns = b_ref.shape[1]
        for start in range(0, columns, 256):
            width = min(256, columns - start)
            acc = None
            for k in range(depth):
                part = lax.dot_general(
                    a_ref[:, k].reshape(chunks * 128, a_ref.shape[3]),
                    b_ref[k, start : start + width],
                    (((1,), (1,)), ((), ())),
                    preferred_element_type=F32,
                )
                acc = part if acc is None else acc + part
            acc = acc.reshape(chunks, 2, 4, 16, width)
            low, high = acc[:, 0], acc[:, 1]
            keep = jnp.where(me == 0, low, high)
            send = jnp.where(me == 0, high, low)
            for n in range(chunks):
                for c in range(width // 128):
                    at = base + n * (columns // 128) + start // 128 + c
                    span = slice(c * 128, (c + 1) * 128)
                    keep_ref[:, at] = keep[n, :, :, span]
                    send_ref[:, at] = send[n, :, :, span]


def product(core, left, right, pairs):
    jobs, base = [], 0
    for li, ri in pairs:
        jobs.append((li, ri, base))
        count = left[li].shape[0] * (right[ri].shape[1] // 128)
        base += count
    half = jax.ShapeDtypeStruct((4, base, 16, 128), F32)
    vmem = pl.BlockSpec(memory_space=pltpu.VMEM)
    return pl.pallas_call(
        functools.partial(product_kernel, jobs, len(left), len(right)),
        out_shape=(half, half),
        in_specs=[pl.BlockSpec(memory_space=pltpu.SMEM)] + [vmem] * (len(left) + len(right)),
        out_specs=(vmem, vmem),
        compiler_params=pltpu.CompilerParams(vmem_limit_bytes=40 * 2**20),
        cost_estimate=pl.CostEstimate(flops=1, bytes_accessed=1, transcendentals=0),
    )(core, *left, *right)


def reduce_chip(keep, send):
    got = permute(send, "core", lambda s: 1 - s)
    mine = place_on("x")
    spots = [mine, (mine + 1) & 3, (mine + 2) & 3, (mine + 3) & 3]
    return [take(keep, at) + take(got, at) for at in spots]


def reduce_x(parts):
    moved = [permute(parts[r], "x", lambda s, r=r: (s + r) % 4) for r in (1, 2, 3)]
    return parts[0] + moved[0] + moved[1] + moved[2]


def exchange_ring(parts, axis):
    moved = [parts[0]] + [permute(parts[r], axis, lambda s, r=r: (s + r) % 4) for r in (1, 2, 3)]
    ring = jnp.stack(moved[::-1] + moved[::-1])
    return lax.dynamic_slice_in_dim(ring, 3 - place_on(axis), 4)


def place_on(axis):
    return lax.axis_index(axis).astype(jnp.uint32)


def take(value, at):
    return lax.dynamic_index_in_dim(value, at, 0, keepdims=False)


def tie(first, second):
    return lax.optimization_barrier((first, second))[0]


def reduce_z(total):
    tiles = total.shape[0]
    value = total.reshape(tiles, 2, 2, 2, 2, 128)
    value = value.transpose(2, 4, 3, 0, 1, 5).reshape(2, 2, 2, tiles * 2, 128)
    for axis in Z[::-1]:
        mine = place_on(axis)
        keep, send = take(value, mine), take(value, 1 - mine)
        got = permute(send, axis, lambda s: 1 - s)
        value = keep + got if axis != Z[0] else None
    return keep, got


def assemble_kernel(places, *refs):
    out_ref = refs[-1]
    for n, place in enumerate(places):
        keep_ref, got_ref = refs[2 * n : 2 * n + 2]
        for m, (rs, rt, cs, ct) in enumerate(place):
            at = (cs * 5 + ct) * 128
            for i in range(2):
                row = slice(2 * m + i, 2 * m + i + 1)
                value = keep_ref[row, :] + got_ref[row, :]
                out_ref[i, rs * 5 + rt : rs * 5 + rt + 1, at : at + 128] = value


def assemble(places, pieces):
    flat = [v for pair in pieces for v in pair]
    vmem = pl.BlockSpec(memory_space=pltpu.VMEM)
    return pl.pallas_call(
        functools.partial(assemble_kernel, places),
        out_shape=jax.ShapeDtypeStruct((2, 10, 1280), F32),
        in_specs=[vmem] * len(flat),
        out_specs=vmem,
        cost_estimate=pl.CostEstimate(flops=1, bytes_accessed=1, transcendentals=0),
    )(*flat)


def body(amplitudes, integrals, screen, occ_energy, vir_energy, owner):
    core = lax.axis_index("core").astype(jnp.int32).reshape(1)
    mask = jnp.repeat(screen, 64, axis=3).astype(jnp.bfloat16)

    own_right = integrals.transpose(0, 2, 3, 1).reshape(4, 640, 640)
    far_right = permute(own_right, "y", lambda s: 3 - s)
    own_left = prepare(amplitudes, mask, 0, 5)
    far_left = permute(own_left, "y", lambda s: s ^ 1)

    def cells_of(row_source, col_source):
        return [(row_source, r, col_source, c) for r in range(5) for c in range(5)]

    def block(left, right):
        pairs = [(l, r) for l in range(len(left)) for r in range(len(right))]
        keep, send = product(core, left, right, pairs)
        return keep, reduce_chip(keep, send)

    total = reduce_x(block([own_left], [own_right])[1])
    pieces = [reduce_z(total)]
    turn = (lax.axis_index("y") + jnp.arange(4)) & 3
    combo = jnp.sum(jnp.where(turn[:, None] == jnp.arange(4)[None], owner[None], 0), axis=1)
    wanted = jnp.stack([combo, 2 * (combo & 1) + (combo >> 1)], axis=1)[:, :, None, None]
    mine = combo[:1]
    first = jnp.where(mine < 2, occ_energy[:1], occ_energy[1:])
    second = jnp.where((mine & 1) == 0, occ_energy[:1], occ_energy[1:])
    row_energy = lax.dynamic_slice_in_dim(vir_energy, place_on(ALL) * 20, 20)
    base = (first + second)[:, None] - row_energy[:, None]
    far_right, base, wanted = lax.optimization_barrier((far_right, base, wanted, pieces[0][0]))[:3]
    keep, parts_a = block([own_left], [far_right])
    total_a = reduce_x(parts_a)
    far_left = tie(far_left, keep)
    total_b = reduce_x(block([far_left], [own_right, far_right])[1])
    pieces.append(reduce_z(jnp.concatenate([total_a, total_b])))
    places = [cells_of(0, 0), cells_of(0, 1) + cells_of(1, 0) + cells_of(1, 1)]
    full = assemble(places, pieces)
    full = full.reshape(2, 10, 2, 2, 320)

    by_pair = [full[i, :, :, j].reshape(10, 640) for i in range(2) for j in range(2)]
    got = jnp.where(
        wanted < 2,
        jnp.where(wanted == 0, by_pair[0], by_pair[1]),
        jnp.where(wanted == 2, by_pair[2], by_pair[3]),
    ).reshape(4, 20, 640)
    got = exchange_ring(got, "y").reshape(4, 2, 2, 5, 2, 320)
    cells = (
        ((0, 0), (1, 0), (1, 1), (0, 1)),
        ((3, 1), (2, 1), (2, 0), (3, 0)),
    )
    rows = []
    for q in range(4):
        cols = [
            got[source, :, 0 if source == q else 1, :, side] for source, side in cells[q // 2]
        ]
        rows.append(jnp.concatenate(cols, axis=-1))
    rows = jnp.stack(rows, axis=1)
    swapped = rows[1].reshape(20, 1280)
    swapped = swapped.reshape(20, 64, 20).transpose(1, 0, 2).reshape(64, 400)
    home, swapped = lax.optimization_barrier((rows[0], swapped))
    mirrored = lax.all_to_all(swapped, ALL, split_axis=0, concat_axis=0, tiled=True)
    mirrored = mirrored.reshape(4, 2, 8, 4, 5, 20).transpose(5, 3, 1, 2, 4, 0).reshape(20, 1280)
    me = place_on(("zh", "zm"))
    direct = exchange_ring([take(home, (me + r) & 3) for r in range(4)], ("zh", "zm"))
    direct = direct.transpose(1, 0, 2).reshape(20, 1280)

    gap = base - vir_energy[None, :]
    return ((direct + mirrored) / gap)[None]


def solution(mesh):
    fine = Mesh(mesh.devices.reshape(2, 2, 2, 4, 2, 4), AXES)
    vir = ("zm", "zp", "x", "core")
    return jax.shard_map(
        body,
        mesh=fine,
        in_specs=(
            P(None, "y", vir, "zh"),
            P(vir, "zh", None, "y"),
            P(None, "y", vir, "zh"),
            P(),
            P(),
            P(),
        ),
        out_specs=P("y", ALL, None),
        check_vma=False,
    )
```

```python
import functools

import jax
import jax.numpy as jnp
from jax import lax
from jax.experimental import pallas as pl
from jax.experimental.pallas import tpu as pltpu
from jax.sharding import Mesh, PartitionSpec as P

AXES = ("zh", "zm", "zp", "x", "core", "y")
Z = ("zh", "zm", "zp")
ALL = ("zh", "zm", "zp", "x", "core")
F32 = jnp.float32


def permute(value, axis, target):
    return lax.ppermute(value, axis, [(s, target(s)) for s in range(lax.axis_size(axis))])


def prepare_kernel(chunks, mask_ref, rows_ref, out_ref):
    for n, t in enumerate(chunks):

        @pl.when(pl.program_id(0) == n)
        def _(t=t):
            for x in range(4):
                for core in range(2):
                    group = []
                    for i in range(2):
                        for zp in range(2):
                            tile = (zp * 160 + (x * 2 + core) * 20 + 4 * t) // 64
                            value = rows_ref[i, zp, x * 2 + core, 0] * mask_ref[i, tile][None]
                            group.append(value.astype(F32))
                    value = jnp.transpose(jnp.concatenate(group, 0), (1, 0, 2))
                    value = value.astype(jnp.bfloat16)
                    at = core * 64 + x * 16
                    for k in range(value.shape[0]):
                        out_ref[0, k, at : at + 16, :] = value[k]


def prepare(amplitudes, mask, lo, hi):
    return pl.pallas_call(
        functools.partial(prepare_kernel, tuple(range(lo, hi))),
        grid=(hi - lo,),
        out_shape=jax.ShapeDtypeStruct((hi - lo, 4, 128, 640), jnp.bfloat16),
        in_specs=[
            pl.BlockSpec((2, 5, 4, 640), lambda t: (0, 0, 0, 0)),
            pl.BlockSpec((2, 2, 8, 1, 4, 4, 640), lambda t: (0, 0, 0, t + lo, 0, 0, 0)),
        ],
        out_specs=pl.BlockSpec((1, 4, 128, 640), lambda t: (t, 0, 0, 0)),
        compiler_params=pltpu.CompilerParams(vmem_limit_bytes=40 * 2**20),
        cost_estimate=pl.CostEstimate(flops=1, bytes_accessed=1, transcendentals=0),
    )(mask, amplitudes.reshape(2, 2, 8, 5, 4, 4, 640))


def product_kernel(jobs, n_left, n_right, core_ref, *refs):
    left = refs[:n_left]
    right = refs[n_left : n_left + n_right]
    keep_ref, send_ref = refs[n_left + n_right :]
    me = core_ref[0]
    for li, ri, base in jobs:
        a_ref, b_ref = left[li], right[ri]
        chunks, depth = a_ref.shape[0], a_ref.shape[1]
        columns = b_ref.shape[1]
        for start in range(0, columns, 256):
            width = min(256, columns - start)
            acc = None
            for k in range(depth):
                part = lax.dot_general(
                    a_ref[:, k].reshape(chunks * 128, a_ref.shape[3]),
                    b_ref[k, start : start + width],
                    (((1,), (1,)), ((), ())),
                    preferred_element_type=F32,
                )
                acc = part if acc is None else acc + part
            acc = acc.reshape(chunks, 2, 4, 16, width)
            low, high = acc[:, 0], acc[:, 1]
            keep = jnp.where(me == 0, low, high)
            send = jnp.where(me == 0, high, low)
            for n in range(chunks):
                for c in range(width // 128):
                    at = base + n * (columns // 128) + start // 128 + c
                    span = slice(c * 128, (c + 1) * 128)
                    keep_ref[:, at] = keep[n, :, :, span]
                    send_ref[:, at] = send[n, :, :, span]


def product(core, left, right, pairs):
    jobs, base = [], 0
    for li, ri in pairs:
        jobs.append((li, ri, base))
        count = left[li].shape[0] * (right[ri].shape[1] // 128)
        base += count
    half = jax.ShapeDtypeStruct((4, base, 16, 128), F32)
    vmem = pl.BlockSpec(memory_space=pltpu.VMEM)
    return pl.pallas_call(
        functools.partial(product_kernel, jobs, len(left), len(right)),
        out_shape=(half, half),
        in_specs=[pl.BlockSpec(memory_space=pltpu.SMEM)] + [vmem] * (len(left) + len(right)),
        out_specs=(vmem, vmem),
        compiler_params=pltpu.CompilerParams(vmem_limit_bytes=40 * 2**20),
        cost_estimate=pl.CostEstimate(flops=1, bytes_accessed=1, transcendentals=0),
    )(core, *left, *right)


def reduce_chip(keep, send):
    got = permute(send, "core", lambda s: 1 - s)
    mine = place_on("x")
    spots = [mine, (mine + 1) & 3, (mine + 2) & 3, (mine + 3) & 3]
    return got, [take(keep, at) + take(got, at) for at in spots]


def reduce_x(parts):
    moved = [permute(parts[r], "x", lambda s, r=r: (s + r) % 4) for r in (1, 2, 3)]
    return parts[0] + moved[0] + moved[1] + moved[2]


def exchange_ring(parts, axis):
    moved = [parts[0]] + [permute(parts[r], axis, lambda s, r=r: (s + r) % 4) for r in (1, 2, 3)]
    ring = jnp.stack(moved[::-1] + moved[::-1])
    return lax.dynamic_slice_in_dim(ring, 3 - place_on(axis), 4)


def place_on(axis):
    return lax.axis_index(axis).astype(jnp.uint32)


def take(value, at):
    return lax.dynamic_index_in_dim(value, at, 0, keepdims=False)


def tie(first, second):
    return lax.optimization_barrier((first, second))[0]


def reduce_z(total):
    tiles = total.shape[0]
    value = total.reshape(tiles, 2, 2, 2, 2, 128)
    value = value.transpose(2, 4, 3, 0, 1, 5).reshape(2, 2, 2, tiles * 2, 128)
    for axis in Z[::-1]:
        mine = place_on(axis)
        keep, send = take(value, mine), take(value, 1 - mine)
        got = permute(send, axis, lambda s: 1 - s)
        value = keep + got if axis != Z[0] else None
    return keep, got


def assemble_kernel(places, *refs):
    out_ref = refs[-1]
    for n, place in enumerate(places):
        keep_ref, got_ref = refs[2 * n : 2 * n + 2]
        for m, (rs, rt, cs, ct) in enumerate(place):
            at = (cs * 5 + ct) * 128
            for i in range(2):
                row = slice(2 * m + i, 2 * m + i + 1)
                value = keep_ref[row, :] + got_ref[row, :]
                out_ref[i, rs * 5 + rt : rs * 5 + rt + 1, at : at + 128] = value


def assemble(places, pieces):
    flat = [v for pair in pieces for v in pair]
    vmem = pl.BlockSpec(memory_space=pltpu.VMEM)
    return pl.pallas_call(
        functools.partial(assemble_kernel, places),
        out_shape=jax.ShapeDtypeStruct((2, 10, 1280), F32),
        in_specs=[vmem] * len(flat),
        out_specs=vmem,
        cost_estimate=pl.CostEstimate(flops=1, bytes_accessed=1, transcendentals=0),
    )(*flat)


def body(amplitudes, integrals, screen, occ_energy, vir_energy, owner):
    core = lax.axis_index("core").astype(jnp.int32).reshape(1)
    mask = jnp.repeat(screen, 64, axis=3).astype(jnp.bfloat16)

    own_right = integrals.transpose(0, 2, 3, 1).reshape(4, 640, 640)
    far_right = permute(own_right, "y", lambda s: 3 - s)
    own_left = prepare(amplitudes, mask, 0, 5)
    far_left = permute(own_left, "y", lambda s: s ^ 1)

    def cells_of(row_source, col_source):
        return [(row_source, r, col_source, c) for r in range(5) for c in range(5)]

    def block(left, right):
        pairs = [(l, r) for l in range(len(left)) for r in range(len(right))]
        keep, send = product(core, left, right, pairs)
        return reduce_chip(keep, send)

    total = reduce_x(block([own_left], [own_right])[1])
    pieces = [reduce_z(total)]
    turn = (lax.axis_index("y") + jnp.arange(4)) & 3
    combo = jnp.sum(jnp.where(turn[:, None] == jnp.arange(4)[None], owner[None], 0), axis=1)
    wanted = jnp.stack([combo, 2 * (combo & 1) + (combo >> 1)], axis=1)[:, :, None, None]
    mine = combo[:1]
    first = jnp.where(mine < 2, occ_energy[:1], occ_energy[1:])
    second = jnp.where((mine & 1) == 0, occ_energy[:1], occ_energy[1:])
    row_energy = lax.dynamic_slice_in_dim(vir_energy, place_on(ALL) * 20, 20)
    base = (first + second)[:, None] - row_energy[:, None]
    far_right, base, wanted = lax.optimization_barrier((far_right, base, wanted, pieces[0][0]))[:3]
    got_a, parts_a = block([own_left], [far_right])
    total_a = reduce_x(parts_a)
    far_left = tie(far_left, got_a)
    total_b = reduce_x(block([far_left], [own_right, far_right])[1])
    pieces.append(reduce_z(jnp.concatenate([total_a, total_b])))
    places = [cells_of(0, 0), cells_of(0, 1) + cells_of(1, 0) + cells_of(1, 1)]
    full = assemble(places, pieces)
    full = full.reshape(2, 10, 2, 2, 320)

    by_pair = [full[i, :, :, j].reshape(10, 640) for i in range(2) for j in range(2)]
    got = jnp.where(
        wanted < 2,
        jnp.where(wanted == 0, by_pair[0], by_pair[1]),
        jnp.where(wanted == 2, by_pair[2], by_pair[3]),
    ).reshape(4, 20, 640)
    got = exchange_ring(got, "y").reshape(4, 2, 2, 5, 2, 320)
    cells = (
        ((0, 0), (1, 0), (1, 1), (0, 1)),
        ((3, 1), (2, 1), (2, 0), (3, 0)),
    )
    rows = []
    for q in range(4):
        cols = [
            got[source, :, 0 if source == q else 1, :, side] for source, side in cells[q // 2]
        ]
        rows.append(jnp.concatenate(cols, axis=-1))
    rows = jnp.stack(rows, axis=1)
    swapped = rows[1].reshape(20, 1280)
    swapped = swapped.reshape(20, 64, 20).transpose(1, 0, 2).reshape(64, 400)
    home, swapped = lax.optimization_barrier((rows[0], swapped))
    mirrored = lax.all_to_all(swapped, ALL, split_axis=0, concat_axis=0, tiled=True)
    mirrored = mirrored.reshape(4, 2, 8, 4, 5, 20).transpose(5, 3, 1, 2, 4, 0).reshape(20, 1280)
    me = place_on(("zh", "zm"))
    direct = exchange_ring([take(home, (me + r) & 3) for r in range(4)], ("zh", "zm"))
    direct = direct.transpose(1, 0, 2).reshape(20, 1280)

    gap = base - vir_energy[None, :]
    return ((direct + mirrored) / gap)[None]


def solution(mesh):
    fine = Mesh(mesh.devices.reshape(2, 2, 2, 4, 2, 4), AXES)
    vir = ("zm", "zp", "x", "core")
    return jax.shard_map(
        body,
        mesh=fine,
        in_specs=(
            P(None, "y", vir, "zh"),
            P(vir, "zh", None, "y"),
            P(None, "y", vir, "zh"),
            P(),
            P(),
            P(),
        ),
        out_specs=P("y", ALL, None),
        check_vma=False,
    )
```
